32 devices in a mesh: group: 2 (over x), expert: 16 (over z, y, core).
Axes of the slice: x: 2, y: 2, z: 4, core: 2. Of those that a mesh axis runs over, the one named last changes fastest.
Arguments:
- tokens: bfloat16 [4096, 7168], P(('group', 'expert')), parts along dimension 0, may hold values from -6 to 6
- expert_ids: int32 [4096, 2], P(('group', 'expert')), parts along dimension 0, may hold values from 0 to 7, all different within a row; in each aligned block of 128 rows (0 to 127, 128 to 255, ...) at most 64 rows name the same one
- gate_weights: float32 [4096, 2], P(('group', 'expert')), parts along dimension 0, may hold values from 0.05 to 1
- slot_expert: int32 [16], replicated, may hold values from 0 to 7, as said below
- w_gate_up: bfloat16 [16, 7168, 1024], P('expert'), may hold values from -0.0625 to 0.0625
- w_down: bfloat16 [16, 512, 7168], P('expert'), may hold values from -0.1875 to 0.1875
Outputs:
- moe_output: bfloat16 [4096, 7168], P(('group', 'expert')), parts along dimension 0
The draws below stay inside these ranges and needn't reach their ends.
There are 2 independent parts, one for each index of `group`. The reference program is written for one: setup_inputs(seed, part) draws one part's arguments, and reference() takes and returns one part's arrays. A program takes and returns all parts, laid end to end along the dimension named above; an argument that names none is the same for every part. Nothing has to cross between parts.
Inputs may be any that keep to these rules, and one draw needn't show every extreme that they name: `expert_ids`: each token names 2 different experts. In the rows of one device (128 tokens) no expert is named more than 64 times, a bound that some block reaches. `slot_expert`: the first 8 slots hold every expert once, and slot s + 8 holds the same expert as slot s.
All inputs are finite; a program needn't handle non-finite values.
Results may differ from the reference program's by a relative error of at most 0.0065.
Values may be sent and summed in bfloat16 or wider, within the bound.
No kernel may reach another device: no remote copies, remote signals or barrier semaphores. Data moves between devices by JAX's collectives and lax.ppermute only.
A program may use at most 128 MiB of HBM per device.

```python
import math
import jax
import jax.numpy as jnp
import numpy as np
from jax import lax

D = 7168
FF = 1024
TOP = 2
TOK_DEV = 128
FSH = 512
EXPERTS = 8
MOST = 64
TOKENS = 2048
N_EXPERT = 16


def draw_slot_expert(key, part):
    order = jax.random.permutation(key, EXPERTS).astype(jnp.int32)
    return jnp.concatenate([order, order])


def block_levels(own_key, dims, cuts, least, high):
    factor_of = 1.0
    for position, parts in cuts:
        heights = jax.random.uniform(jax.random.fold_in(jax.random.fold_in(own_key, 6), position), (parts,), jnp.float32, least / len(cuts), high / len(cuts))
        factor_of = factor_of * jnp.repeat(jnp.exp(heights), dims[position] // parts).reshape((-1,) + (1,) * (len(dims) - 1 - position))
    return factor_of


def deal_out(own_key, own, number, rows, amount, top, most, lean):
    ranking = jax.random.permutation(own_key, amount)
    heavy_load, usual = load_shares(amount, rows * top, most, lean, True), load_shares(amount, rows * top, most, lean, False)
    places = jnp.arange(amount)

    def named(sizes, rotation):
        used = int((sizes > 0).sum())
        fixed = max(1, used // 4)
        passed = fixed + (places - fixed + rotation * (used - fixed)) % max(1, amount - fixed)
        return jnp.zeros((amount,), jnp.int32).at[ranking[jnp.where(places < fixed, places, passed)]].set(jnp.asarray(sizes, jnp.int32))

    sizes = jnp.where(number % 4 == 0, named(heavy_load, number // 4), named(usual, number - number // 4 - 1))
    mixed = jax.random.permutation(jax.random.fold_in(own, 3), amount)
    donor, taker = mixed[0:amount // 2 * 2:2], mixed[1:amount // 2 * 2:2]
    room = jnp.minimum(sizes[donor] - 1, most - sizes[taker]) // 2
    room = jnp.where((donor == ranking[0]) | (taker == ranking[0]) | (sizes[taker] == 0), 0, jnp.maximum(room, 0))
    passed = jax.random.randint(jax.random.fold_in(own, 4), (amount // 2,), 0, 1 << 20) % (room + 1)
    sizes = sizes.at[donor].add(-passed).at[taker].add(passed)
    members = jnp.searchsorted(jnp.cumsum(sizes), jnp.arange(rows * top), side="right").astype(jnp.int32)
    grid = members.reshape(top, rows).T
    grid = grid[jax.random.permutation(jax.random.fold_in(own, 1), rows)]
    rotation = jax.random.randint(jax.random.fold_in(own, 2), (rows, 1), 0, top)
    return jnp.take_along_axis(grid, (jnp.arange(top)[None, :] + rotation) % top, axis=1)


def load_shares(count, total, reach, skew, full):
    loads = [(1 << 20) // math.isqrt(rank ** skew) + 1 for rank in range(1, count + 1)]
    largest = reach if full else min(reach, max(-(-total // count), total * loads[0] // sum(loads)))
    least = 1 if total - largest >= count - 1 else 0
    given, rest = [largest] + [least] * (count - 1), total - largest - least * (count - 1)
    while rest > 0:
        free = [i for i in range(1, count) if given[i] < largest] or [i for i in range(1, count) if given[i] < reach]
        mass, remaining = sum([loads[i] for i in free]), rest
        for i in free:
            more = min(reach - given[i], max(1, remaining * loads[i] // mass), rest)
            given[i] = given[i] + more
            rest = rest - more
    return np.array(given)


def scatter_about(stream_key, extent, scale, most, split=(), kind=jnp.bfloat16):
    drawn = jax.random.normal(stream_key, extent, jnp.float32) * scale
    if len(split) > 0:
        drawn = block_levels(stream_key, extent, split, -0.22, 0.18) * drawn
    return jnp.clip(drawn, min=-most, max=most).astype(kind)


def setup_inputs(seed: int = 0, part: int = 0) -> dict:
    key_list = jax.random.split(jax.random.key(seed), 7)
    own_keys = jax.random.split(jax.random.fold_in(key_list[6], part), 7)
    tokens = scatter_about(own_keys[0], (TOKENS, D), 1.0, 6.0, ((0, 16),))
    expert_ids_keys = jax.random.split(jax.random.fold_in(own_keys[1], 1), TOKENS // TOK_DEV)
    expert_ids_turns = jax.random.permutation(jax.random.fold_in(own_keys[1], 3), TOKENS // TOK_DEV)
    expert_ids = jax.vmap(lambda own, number: deal_out(jax.random.fold_in(own_keys[1], 2), own, number, TOK_DEV, EXPERTS, TOP, MOST, 2))(expert_ids_keys, expert_ids_turns).reshape((TOKENS, TOP))
    gate_weights = jnp.clip(jnp.exp(math.log(1.0) - 2.9957323 * jax.random.uniform(own_keys[2], (TOKENS, TOP), jnp.float32) ** block_levels(own_keys[2], (TOKENS, TOP), ((0, 16),), -0.2, 0.2)), 0.05, 1.0)
    slot_expert = draw_slot_expert(jax.random.fold_in(key_list[6], 71), part)
    w_gate_up = scatter_about(key_list[4], (N_EXPERT, D, FF), D ** -0.5, 0.0625, ((0, 16),))
    w_down = scatter_about(key_list[5], (N_EXPERT, FSH, D), FF ** -0.5, 0.1875, ((0, 16),))
    return dict(tokens=tokens, expert_ids=expert_ids, gate_weights=gate_weights, slot_expert=slot_expert, w_gate_up=w_gate_up, w_down=w_down)


def reference(tokens, expert_ids, gate_weights, slot_expert, w_gate_up, w_down):
    choice_total = TOKENS * TOP
    span = N_EXPERT * MOST
    flat_ids = expert_ids.reshape(-1).astype(jnp.int32)
    order = jnp.argsort(flat_ids, stable=True).astype(jnp.int32)
    member = (flat_ids[:, None] == jnp.arange(EXPERTS, dtype=jnp.int32)[None, :]).astype(jnp.int32)
    counts = jnp.sum(member, axis=0).astype(jnp.int32)
    starts = (jnp.cumsum(counts) - counts).astype(jnp.int32)
    padded_order = jnp.concatenate([order, jnp.zeros((span,), jnp.int32)])

    def slot_half(rows, slot):
        projected = jnp.dot(rows, w_gate_up[slot], preferred_element_type=jnp.float32)
        hidden = (jax.nn.silu(projected[:, :FSH]) * projected[:, FSH:]).astype(jnp.bfloat16)
        return jnp.dot(hidden, w_down[slot], preferred_element_type=jnp.float32).astype(jnp.bfloat16)

    def one_expert(slot):
        expert = slot_expert[slot]
        picked = lax.dynamic_slice_in_dim(padded_order, starts[expert], span)
        valid = jnp.arange(span, dtype=jnp.int32) < counts[expert]
        rows = tokens[picked // TOP]
        lower = slot_half(rows, slot)
        upper = slot_half(rows, slot + EXPERTS)
        summed = (lower.astype(jnp.float32) + upper.astype(jnp.float32)).astype(jnp.bfloat16)
        summed = jnp.where(valid[:, None], summed, jnp.zeros_like(summed))
        target = jnp.where(valid, picked, choice_total).astype(jnp.int32)
        return summed, target

    outputs, targets = lax.map(one_expert, jnp.arange(EXPERTS, dtype=jnp.int32))
    table = jnp.zeros((choice_total + 1, D), jnp.bfloat16)
    table = table.at[targets.reshape(-1)].set(outputs.reshape(-1, D))
    chosen = table[:choice_total].reshape(TOKENS, TOP, D)
    total = jnp.sum(gate_weights[:, :, None] * chosen.astype(jnp.float32), axis=1)
    return total.astype(jnp.bfloat16)
```

```python
import jax
import jax.numpy as jnp
from jax import lax
from jax.sharding import PartitionSpec as P

PIECES = ((2, "y"), (2, "z"), (2, "y"), (2, "y"))


def pairs_core(devices):
    return [(i, i ^ 1) for i in range(devices)]


def pairs_column(devices):
    return [(i, i ^ 2) for i in range(devices)]


def pairs_line(devices, step, far):
    planes = devices // 4
    return [
        (i, i + 4 * step) for i in range(devices) if 0 <= i // 4 + step * far < planes
    ]


def add32(*terms):
    total = terms[0].astype(jnp.float32)
    for term in terms[1:]:
        total = total + term.astype(jnp.float32)
    return total


def line_sum(terms, devices):
    planes = devices // 4
    arrived = []
    for step in (1, -1):
        running = None
        for far in range(planes - 1, 0, -1):
            mine = terms[planes - far] if step == 1 else terms[far]
            if running is not None:
                mine = add32(mine, running).astype(jnp.bfloat16)
            running = lax.ppermute(mine, "expert", pairs_line(devices, step, far))
        arrived.append(running)
    return add32(terms[0], *arrived)


def per_device(tokens, expert_ids, gate_weights, slot_expert, w_gate_up, w_down):
    devices = lax.axis_size("expert")
    planes = devices // 4
    tok_rows, width = tokens.shape
    top_count = expert_ids.shape[1]
    me = lax.axis_index("expert")
    gate_up = w_gate_up[0]
    down = w_down[0]
    half = gate_up.shape[1] // 2

    far = jnp.arange(planes, dtype=jnp.int32)
    plane = jnp.mod(me // 4 - far, planes)
    low = jnp.arange(4, dtype=jnp.int32)
    swap = (low // 2) + 2 * (low % 2)
    low = jnp.bitwise_xor(me % 4, swap)
    order = (plane[None, :] * 4 + low[:, None]).reshape(-1)

    routing = jnp.concatenate(
        [expert_ids.T.astype(jnp.float32), gate_weights.T], axis=0
    )
    routing = lax.all_gather(routing, "expert", axis=0, tiled=False)
    mine = slot_expert[me].astype(jnp.float32)
    gate = jnp.sum(
        jnp.where(routing[:, :top_count] == mine, routing[:, top_count:], 0.0), axis=1
    )
    pick = (order[:, None] == jnp.arange(devices, dtype=jnp.int32)[None, :])
    gate = jnp.sum(jnp.where(pick[:, :, None], gate[None, :, :], 0.0), axis=1)

    results = []
    at = 0
    for eighths, kind in PIECES:
        rows = tok_rows * eighths // 8
        piece = lax.slice_in_dim(tokens, at, at + rows, axis=0)
        gathered = lax.all_gather(piece, "expert", axis=0, tiled=True)
        projected = jnp.dot(gathered, gate_up, preferred_element_type=jnp.float32)
        hidden = (jax.nn.silu(projected[:, :half]) * projected[:, half:]).astype(jnp.bfloat16)
        hidden = jnp.take(hidden.reshape(devices, rows, half), order, axis=0)
        scale = lax.slice_in_dim(gate, at, at + rows, axis=1)

        def part(first, last):
            product = jnp.dot(
                hidden[first:last].reshape(-1, half), down, preferred_element_type=jnp.float32
            )
            product = product * scale[first:last].reshape(-1, 1)
            return product.astype(jnp.bfloat16).reshape(last - first, rows, width)

        other = part(2 * planes, 4 * planes)
        other = lax.ppermute(other, "expert", pairs_core(devices))
        if kind == "y":
            crossing = add32(part(planes, 2 * planes), other[planes:]).astype(jnp.bfloat16)
            crossing = lax.ppermute(crossing, "expert", pairs_column(devices))
            summed = add32(part(0, planes), other[:planes], crossing).astype(jnp.bfloat16)
            total = line_sum([summed[j] for j in range(planes)], devices)
        else:
            summed = add32(part(0, 2 * planes), other).astype(jnp.bfloat16)
            summed = summed.reshape(2, planes, rows, width)
            total = line_sum([summed[:, j] for j in range(planes)], devices)
            crossing = lax.ppermute(
                total[1].astype(jnp.bfloat16), "expert", pairs_column(devices)
            )
            total = add32(total[0], crossing)
        results.append(total.astype(jnp.bfloat16))
        at += rows
    return jnp.concatenate(results, axis=0)


def solution(mesh):
    return jax.shard_map(
        per_device,
        mesh=mesh,
        in_specs=(
            P(("group", "expert"), None),
            P(("group", "expert"), None),
            P(("group", "expert"), None),
            P(),
            P("expert", None, None),
            P("expert", None, None),
        ),
        out_specs=P(("group", "expert"), None),
        check_vma=False,
    )
```

```python
import jax
import jax.numpy as jnp
from jax import lax
from jax.experimental import pallas as pl
from jax.experimental.pallas import tpu as pltpu
from jax.sharding import PartitionSpec as P

PARTS = (3, 3, 2)
TILE = 256


def pairs_flip(devices, bits):
    return [(i, i ^ bits) for i in range(devices)]


def add32(*terms):
    total = terms[0].astype(jnp.float32)
    for term in terms[1:]:
        total = total + term.astype(jnp.float32)
    return total


def hidden_kernel(place, tokens, weight, gate, out):
    planes, _, rows, width = tokens.shape
    half = weight.shape[1] // 2

    @pl.loop(0, half // TILE)
    def _(n):
        first = pl.ds(pl.multiple_of(n * TILE, TILE), TILE)
        last = pl.ds(pl.multiple_of(half + n * TILE, TILE), TILE)
        x = tokens[:, 0].reshape(planes * rows, width)
        a = jnp.dot(x, weight[:, first], preferred_element_type=jnp.float32)
        b = jnp.dot(x, weight[:, last], preferred_element_type=jnp.float32)
        h = a / (1.0 + jnp.exp(-a)) * b
        h = h.reshape(planes, rows, TILE) * gate[:, 0]
        h = h.astype(out.dtype)
        for plane in range(planes):
            out[0, jnp.bitwise_xor(place[0], plane), :, first] = h[plane]


def hidden_rows(gathered, weight, gate, me, which):
    planes, _, rows, width = gathered.shape
    half = weight.shape[1] // 2
    block = rows // 2
    place = jnp.stack([me // 4, me % 4]).astype(jnp.int32)

    def source(flip, place):
        return (0, jnp.bitwise_xor(place[1], flip), which, 0)

    return pl.pallas_call(
        hidden_kernel,
        out_shape=jax.ShapeDtypeStruct((4, planes, block, half), jnp.bfloat16),
        grid_spec=pltpu.PrefetchScalarGridSpec(
            num_scalar_prefetch=1,
            grid=(4,),
            in_specs=[
                pl.BlockSpec((planes, 1, block, width), source),
                pl.BlockSpec(
                    weight.shape, lambda flip, place: (0, 0), pipeline_mode=pl.Buffered(1)
                ),
                pl.BlockSpec((planes, 1, block, 1), source),
            ],
            out_specs=pl.BlockSpec(
                (1, planes, block, half), lambda flip, place: (flip, 0, 0, 0)
            ),
        ),
        compiler_params=pltpu.CompilerParams(vmem_limit_bytes=44 * 1024 * 1024),
        cost_estimate=pl.CostEstimate(flops=1, bytes_accessed=1, transcendentals=0),
    )(place, gathered, weight, gate)


def per_device(tokens, expert_ids, gate_weights, slot_expert, w_gate_up, w_down):
    devices = lax.axis_size("expert")
    groups = lax.axis_size("group")
    planes = devices // 4
    bits = planes.bit_length() - 1
    tok_rows, width = tokens.shape
    top_count = expert_ids.shape[1]
    me = lax.axis_index("expert")
    gate_up = w_gate_up[0]
    down = w_down[0]
    half = down.shape[0]
    share = half // groups
    shift = lax.axis_index("group") * share
    ring = [(i, (i - 1) % groups) for i in range(groups)]
    tie = lax.optimization_barrier

    def over_core(array):
        return lax.ppermute(array, "expert", pairs_flip(devices, 1))

    def over_column(array):
        return lax.ppermute(array, "expert", pairs_flip(devices, 2))

    def over_groups(array):
        shares = [array]
        for _ in range(groups - 1):
            shares.append(lax.ppermute(shares[-1], "group", ring))
        return jnp.concatenate(shares, axis=0)

    gathered = lax.all_gather(tokens, "expert", axis=0, tiled=True)
    routing = jnp.concatenate(
        [expert_ids.T.astype(jnp.float32), gate_weights.T], axis=0
    )
    routing = lax.all_gather(routing, "expert", axis=0, tiled=False)
    mine = slot_expert[me].astype(jnp.float32)
    gate = jnp.sum(
        jnp.where(routing[:, :top_count] == mine, routing[:, top_count:], 0.0), axis=1
    )
    gate = gate.reshape(planes, 4, tok_rows, 1)

    edges = [width * sum(PARTS[:p]) // 8 for p in range(len(PARTS) + 1)]
    owns = [down[:, edges[p] : edges[p + 1]] for p in range(len(PARTS))]
    own_share = lax.dynamic_slice_in_dim(down, shift, share, axis=0)
    own_shares = [own_share[:, edges[p] : edges[p + 1]] for p in range(len(PARTS))]
    siblings = [over_core(own) for own in owns]
    gathered, gate, siblings, own_shares = tie((gathered, gate, siblings, own_shares))

    def exchange(hidden):
        hidden = hidden.reshape(4, -1, half)
        terms = [hidden[0]]
        for bits in (1, 2, 3):
            term = lax.ppermute(hidden[bits], "expert", pairs_flip(devices, bits))
            if bits >= 2:
                term = lax.dynamic_slice_in_dim(
                    jnp.concatenate([term, term], axis=1), shift, half, axis=1
                )
            terms.append(term)
        return terms

    def second(terms, weight):
        out = 0.0
        for term, block in zip(terms, weight):
            out = out + jnp.dot(term, block, preferred_element_type=jnp.float32)
        return out.astype(jnp.bfloat16).reshape(planes, -1, out.shape[1])

    def send(terms, bit):
        far = sorted((r for r in terms if r >> bit & 1), reverse=True)
        return {r ^ (1 << bit): flip(terms[r], 4 << bit) for r in far}

    def flip(array, mask):
        return lax.ppermute(array, "expert", pairs_flip(devices, mask))

    def add_came(terms, came):
        return {
            r: add32(terms[r], came[r]).astype(jnp.bfloat16) if r else terms[r] for r in came
        }

    def go_near(outs):
        here = [[out[0]] for out in outs]
        held = [dict(enumerate(out)) for out in outs]
        for bit in range(bits - 1):
            came = [send(terms, bit) for terms in held]
            held = [add_came(terms, moved) for terms, moved in zip(held, came)]
            for some, moved in zip(here, came):
                some.append(moved[0])
        return [terms[1 << (bits - 1)] for terms in held], here

    gathered = gathered.reshape(planes, 4, tok_rows, width)
    columns = [over_column(own_shares[p]) for p in range(2)]
    hidden = hidden_rows(gathered, gate_up, gate, me, 0)
    hidden, columns[0], gathered = tie((hidden, columns[0], gathered))
    columns[0] = over_groups(columns[0])
    terms = [exchange(hidden)]
    hidden = hidden_rows(gathered, gate_up, gate, me, 1)
    hidden, columns, terms = tie((hidden, columns, terms))
    both = over_core(columns[0])
    column = over_groups(columns[1])
    terms.append(exchange(hidden))
    terms, both, own_shares = tie((terms, both, own_shares))
    later = over_column(own_shares[2])

    last = 4 << (bits - 1)
    weight = (owns[0], siblings[0], columns[0], both)
    outs = [second(term, weight) for term in terms]
    results = []
    before = None
    for p in range(len(PARTS)):
        more = p + 1 < len(PARTS)
        sums, here = go_near(outs)
        if more:
            sums, column, before = tie((sums, column, before))
        else:
            sums, before = tie((sums, before))
        if before is not None:
            results.append(before)
        before = ([flip(rows, last) for rows in sums], here)
        if more:
            weight = (owns[p + 1], siblings[p + 1], column, over_core(column))
            outs = [second(term, weight) for term in terms]
            if p + 2 < len(PARTS):
                outs, later = tie((outs, later))
                column = over_groups(later)
    results.append(before)
    columns = []
    for crossing, here in results:
        totals = [add32(*some, came).astype(jnp.bfloat16) for some, came in zip(here, crossing)]
        columns.append(jnp.concatenate(totals, axis=0))
    return jnp.concatenate(columns, axis=1)


def solution(mesh):
    return jax.shard_map(
        per_device,
        mesh=mesh,
        in_specs=(
            P(("group", "expert"), None),
            P(("group", "expert"), None),
            P(("group", "expert"), None),
            P(),
            P("expert", None, None),
            P("expert", None, None),
        ),
        out_specs=P(("group", "expert"), None),
        check_vma=False,
    )
```

```python
import jax
import jax.numpy as jnp
from jax import lax
from jax.experimental import pallas as pl
from jax.experimental.pallas import tpu as pltpu
from jax.sharding import PartitionSpec as P

PARTS = (3, 3, 2)
AHEAD = 2
TILE = 256


def pairs_flip(devices, bits):
    return [(i, i ^ bits) for i in range(devices)]


def add32(*terms):
    total = terms[0].astype(jnp.float32)
    for term in terms[1:]:
        total = total + term.astype(jnp.float32)
    return total


def hidden_kernel(place, tokens, weight, gate, out):
    planes, _, rows, width = tokens.shape
    half = weight.shape[1] // 2

    @pl.loop(0, half // TILE)
    def _(n):
        first = pl.ds(pl.multiple_of(n * TILE, TILE), TILE)
        last = pl.ds(pl.multiple_of(half + n * TILE, TILE), TILE)
        x = tokens[:, 0].reshape(planes * rows, width)
        a = jnp.dot(x, weight[:, first], preferred_element_type=jnp.float32)
        b = jnp.dot(x, weight[:, last], preferred_element_type=jnp.float32)
        h = a / (1.0 + jnp.exp(-a)) * b
        h = h.reshape(planes, rows, TILE) * gate[:, 0]
        h = h.astype(out.dtype)
        for plane in range(planes):
            out[0, jnp.bitwise_xor(place[0], plane), :, first] = h[plane]


def hidden_rows(gathered, weight, gate, me, which):
    planes, _, rows, width = gathered.shape
    half = weight.shape[1] // 2
    block = rows // 2
    place = jnp.stack([me // 4, me % 4]).astype(jnp.int32)

    def source(flip, place):
        return (0, jnp.bitwise_xor(place[1], flip), which, 0)

    return pl.pallas_call(
        hidden_kernel,
        out_shape=jax.ShapeDtypeStruct((4, planes, block, half), jnp.bfloat16),
        grid_spec=pltpu.PrefetchScalarGridSpec(
            num_scalar_prefetch=1,
            grid=(4,),
            in_specs=[
                pl.BlockSpec((planes, 1, block, width), source),
                pl.BlockSpec(
                    weight.shape, lambda flip, place: (0, 0), pipeline_mode=pl.Buffered(1)
                ),
                pl.BlockSpec((planes, 1, block, 1), source),
            ],
            out_specs=pl.BlockSpec(
                (1, planes, block, half), lambda flip, place: (flip, 0, 0, 0)
            ),
        ),
        compiler_params=pltpu.CompilerParams(vmem_limit_bytes=44 * 1024 * 1024),
        cost_estimate=pl.CostEstimate(flops=4*planes*rows//2*width*2*half*2//1, bytes_accessed=2*width*2*half//1, transcendentals=0),
    )(place, gathered, weight, gate)


def sum_kernel(*refs):
    *pairs, out = refs
    half = len(pairs) // 2
    total = 0.0
    for term, weight in zip(pairs[:half], pairs[half:]):
        total = total + jnp.dot(term[...], weight[...], preferred_element_type=jnp.float32)
    out[...] = total.astype(out.dtype)


def sum_of_products(terms, weights):
    rows, depth = terms[0].shape
    width = weights[0].shape[1]
    tile = max(t for t in range(128, 897, 128) if width % t == 0)
    return pl.pallas_call(
        sum_kernel,
        out_shape=jax.ShapeDtypeStruct((rows, width), jnp.bfloat16),
        grid=(width // tile,),
        in_specs=[pl.BlockSpec((rows, depth), lambda i: (0, 0)) for _ in terms]
        + [pl.BlockSpec((depth, tile), lambda i: (0, i)) for _ in weights],
        out_specs=pl.BlockSpec((rows, tile), lambda i: (0, i)),
        compiler_params=pltpu.CompilerParams(vmem_limit_bytes=32 * 1024 * 1024),
        cost_estimate=pl.CostEstimate(flops=2*rows*4*depth*width//1, bytes_accessed=8*depth*width//1, transcendentals=0),
    )(*terms, *weights)


def per_device(tokens, expert_ids, gate_weights, slot_expert, w_gate_up, w_down):
    devices = lax.axis_size("expert")
    groups = lax.axis_size("group")
    planes = devices // 4
    bits = planes.bit_length() - 1
    tok_rows, width = tokens.shape
    top_count = expert_ids.shape[1]
    me = lax.axis_index("expert")
    gate_up = w_gate_up[0]
    down = w_down[0]
    half = down.shape[0]
    share = half // groups
    shift = lax.axis_index("group") * share
    ring = [(i, (i - 1) % groups) for i in range(groups)]
    tie = lax.optimization_barrier

    def over_core(array):
        return lax.ppermute(array, "expert", pairs_flip(devices, 1))

    def over_column(array):
        return lax.ppermute(array, "expert", pairs_flip(devices, 2))

    gathered = lax.all_gather(tokens, "expert", axis=0, tiled=True)
    routing = jnp.concatenate(
        [expert_ids.T.astype(jnp.float32), gate_weights.T], axis=0
    )
    routing = lax.all_gather(routing, "expert", axis=0, tiled=False)
    mine = slot_expert[me].astype(jnp.float32)
    gate = jnp.sum(
        jnp.where(routing[:, :top_count] == mine, routing[:, top_count:], 0.0), axis=1
    )
    gate = gate.reshape(planes, 4, tok_rows, 1)

    edges = [width * sum(PARTS[:p]) // 8 for p in range(len(PARTS) + 1)]
    owns = [down[:, edges[p] : edges[p + 1]] for p in range(len(PARTS))]
    own_share = lax.dynamic_slice_in_dim(down, shift, share, axis=0)
    own_shares = [own_share[:, edges[p] : edges[p + 1]] for p in range(len(PARTS))]
    siblings = [over_core(own) for own in owns]
    gathered, gate, siblings, own_shares = tie((gathered, gate, siblings, own_shares))

    def exchange(hidden):
        hidden = hidden.reshape(4, -1, half)
        terms = [hidden[0]]
        for bits in (1, 2, 3):
            term = lax.ppermute(hidden[bits], "expert", pairs_flip(devices, bits))
            if bits >= 2:
                term = lax.dynamic_slice_in_dim(
                    jnp.concatenate([term, term], axis=1), shift, half, axis=1
                )
            terms.append(term)
        return terms

    def second(terms, weight):
        return sum_of_products(terms, weight).reshape(planes, tok_rows, -1)

    def send(terms, bit):
        far = sorted((r for r in terms if r >> bit & 1), reverse=True)
        return {r ^ (1 << bit): flip(terms[r], 4 << bit) for r in far}

    def flip(array, mask):
        return lax.ppermute(array, "expert", pairs_flip(devices, mask))

    def add_came(terms, came):
        return {
            r: add32(terms[r], came[r]).astype(jnp.bfloat16) if r else terms[r] for r in came
        }

    def go_near(outs):
        here = [[out[0]] for out in outs]
        held = [dict(enumerate(out)) for out in outs]
        for bit in range(bits - 1):
            came = [send(terms, bit) for terms in held]
            held = [add_came(terms, moved) for terms, moved in zip(held, came)]
            for some, moved in zip(here, came):
                some.append(moved[0])
        return [terms[1 << (bits - 1)] for terms in held], here

    gathered = gathered.reshape(planes, 4, tok_rows, width)
    def halves_sum(out):
        (crossing,), (here,) = go_near([out])
        return crossing, here

    def over_ring(array):
        shares = [array]
        for _ in range(groups - 1):
            shares.append(lax.ppermute(shares[-1], "group", ring))
        return shares

    def joined(shares):
        return jnp.concatenate(shares, axis=0)

    def blocks(p, column):
        return owns[p], siblings[p], column, over_core(column)

    last = 4 << (bits - 1)
    count = len(PARTS)
    crossed = [over_column(own_shares[p]) for p in range(AHEAD)]
    hidden = hidden_rows(gathered, gate_up, gate, me, 0)
    hidden, crossed[0], gathered = tie((hidden, crossed[0], gathered))

    columns = [over_ring(crossed[0])]
    halves = [exchange(hidden)]
    hidden = hidden_rows(gathered, gate_up, gate, me, 1)
    hidden, columns, crossed, halves, own_shares = tie((hidden, columns, crossed, halves, own_shares))

    columns.append(over_ring(crossed[1]))
    if len(crossed) < 3:
        crossed.append(over_column(own_shares[2]))
    halves.append(exchange(hidden))
    terms = [
        jnp.concatenate([part.reshape(planes, -1, half) for part in parts], axis=1).reshape(-1, half)
        for parts in zip(*halves)
    ]
    out = second(terms, blocks(0, joined(columns[0])))

    totals = []
    before = None
    for w in range(count):
        out, columns, crossed, own_shares = tie((out, columns, crossed, own_shares))
        if w + 2 < count:
            columns.append(over_ring(crossed[w + 2]))
        if w + 3 < count:
            crossed.append(over_column(own_shares[w + 3]))
        crossing, here = halves_sum(out)
        if before is not None:
            totals.append(add32(*before).astype(jnp.bfloat16))
        if w + 1 < count:
            out = second(terms, blocks(w + 1, joined(columns[w + 1])))
        crossing, totals, out = tie((crossing, totals, out))
        before = here + [flip(crossing, last)]
    totals.append(add32(*before).astype(jnp.bfloat16))
    return jnp.concatenate(totals, axis=1)


def solution(mesh):
    return jax.shard_map(
        per_device,
        mesh=mesh,
        in_specs=(
            P(("group", "expert"), None),
            P(("group", "expert"), None),
            P(("group", "expert"), None),
            P(),
            P("expert", None, None),
            P("expert", None, None),
        ),
        out_specs=P(("group", "expert"), None),
        check_vma=False,
    )
```

```python
import jax
import jax.numpy as jnp
from jax import lax
from jax.experimental import pallas as pl
from jax.experimental.pallas import tpu as pltpu
from jax.sharding import PartitionSpec as P

PARTS = (3, 3, 2)
AHEAD = 2
TILE = 256


def pairs_flip(devices, bits):
    return [(i, i ^ bits) for i in range(devices)]


def add32(*terms):
    total = terms[0].astype(jnp.float32)
    for term in terms[1:]:
        total = total + term.astype(jnp.float32)
    return total


def hidden_kernel(place, tokens, weight, gate, out):
    planes, _, rows, width = tokens.shape
    half = weight.shape[1] // 2

    @pl.loop(0, half // TILE)
    def _(n):
        first = pl.ds(pl.multiple_of(n * TILE, TILE), TILE)
        last = pl.ds(pl.multiple_of(half + n * TILE, TILE), TILE)
        x = tokens[:, 0].reshape(planes * rows, width)
        a = jnp.dot(x, weight[:, first], preferred_element_type=jnp.float32)
        b = jnp.dot(x, weight[:, last], preferred_element_type=jnp.float32)
        h = a / (1.0 + jnp.exp(-a)) * b
        h = h.reshape(planes, rows, TILE) * gate[:, 0]
        h = h.astype(out.dtype)
        for plane in range(planes):
            out[0, jnp.bitwise_xor(place[0], plane), :, first] = h[plane]


def hidden_rows(gathered, weight, gate, me, which):
    planes, _, rows, width = gathered.shape
    half = weight.shape[1] // 2
    block = rows // 2
    place = jnp.stack([me // 4, me % 4]).astype(jnp.int32)

    def source(flip, place):
        return (0, jnp.bitwise_xor(place[1], flip), which, 0)

    return pl.pallas_call(
        hidden_kernel,
        out_shape=jax.ShapeDtypeStruct((4, planes, block, half), jnp.bfloat16),
        grid_spec=pltpu.PrefetchScalarGridSpec(
            num_scalar_prefetch=1,
            grid=(4,),
            in_specs=[
                pl.BlockSpec((planes, 1, block, width), source),
                pl.BlockSpec(
                    weight.shape, lambda flip, place: (0, 0), pipeline_mode=pl.Buffered(1)
                ),
                pl.BlockSpec((planes, 1, block, 1), source),
            ],
            out_specs=pl.BlockSpec(
                (1, planes, block, half), lambda flip, place: (flip, 0, 0, 0)
            ),
        ),
        compiler_params=pltpu.CompilerParams(vmem_limit_bytes=44 * 1024 * 1024),
        cost_estimate=pl.CostEstimate(flops=4*planes*rows//2*width*2*half*2//1, bytes_accessed=2*width*2*half//1, transcendentals=0),
    )(place, gathered, weight, gate)


def sum_kernel(*refs):
    *pairs, out = refs
    half = len(pairs) // 2
    total = 0.0
    for term, weight in zip(pairs[:half], pairs[half:]):
        total = total + jnp.dot(term[...], weight[...], preferred_element_type=jnp.float32)
    out[...] = total.astype(out.dtype)


def sum_of_products(terms, weights):
    rows, depth = terms[0].shape
    width = weights[0].shape[1]
    tile = max(t for t in range(128, 897, 128) if width % t == 0)
    return pl.pallas_call(
        sum_kernel,
        out_shape=jax.ShapeDtypeStruct((rows, width), jnp.bfloat16),
        grid=(width // tile,),
        in_specs=[pl.BlockSpec((rows, depth), lambda i: (0, 0)) for _ in terms]
        + [pl.BlockSpec((depth, tile), lambda i: (0, i)) for _ in weights],
        out_specs=pl.BlockSpec((rows, tile), lambda i: (0, i)),
        compiler_params=pltpu.CompilerParams(vmem_limit_bytes=32 * 1024 * 1024),
        cost_estimate=pl.CostEstimate(flops=2*rows*4*depth*width//1, bytes_accessed=8*depth*width//1, transcendentals=0),
    )(*terms, *weights)


def per_device(tokens, expert_ids, gate_weights, slot_expert, w_gate_up, w_down):
    devices = lax.axis_size("expert")
    groups = lax.axis_size("group")
    planes = devices // 4
    bits = planes.bit_length() - 1
    tok_rows, width = tokens.shape
    top_count = expert_ids.shape[1]
    me = lax.axis_index("expert")
    gate_up = w_gate_up[0]
    down = w_down[0]
    half = down.shape[0]
    share = half // groups
    shift = lax.axis_index("group") * share
    ring = [(i, (i - 1) % groups) for i in range(groups)]
    tie = lax.optimization_barrier

    def over_core(array):
        return lax.ppermute(array, "expert", pairs_flip(devices, 1))

    def over_column(array):
        return lax.ppermute(array, "expert", pairs_flip(devices, 2))

    gathered = lax.all_gather(tokens, "expert", axis=0, tiled=True)
    routing = jnp.concatenate(
        [expert_ids.T.astype(jnp.float32), gate_weights.T], axis=0
    )
    routing = lax.all_gather(routing, "expert", axis=0, tiled=False)
    mine = slot_expert[me].astype(jnp.float32)
    gate = jnp.sum(
        jnp.where(routing[:, :top_count] == mine, routing[:, top_count:], 0.0), axis=1
    )
    gate = gate.reshape(planes, 4, tok_rows, 1)

    edges = [width * sum(PARTS[:p]) // 8 for p in range(len(PARTS) + 1)]
    owns = [down[:, edges[p] : edges[p + 1]] for p in range(len(PARTS))]
    own_share = lax.dynamic_slice_in_dim(down, shift, share, axis=0)
    own_shares = [own_share[:, edges[p] : edges[p + 1]] for p in range(len(PARTS))]
    siblings = [over_core(own) for own in owns]
    gathered, gate, siblings, own_shares = tie((gathered, gate, siblings, own_shares))

    def exchange(hidden):
        hidden = hidden.reshape(4, -1, half)
        terms = [hidden[0]]
        for bits in (1, 2, 3):
            term = lax.ppermute(hidden[bits], "expert", pairs_flip(devices, bits))
            if bits >= 2:
                term = lax.dynamic_slice_in_dim(
                    jnp.concatenate([term, term], axis=1), shift, half, axis=1
                )
            terms.append(term)
        return terms

    def second(terms, weight):
        return sum_of_products(terms, weight).reshape(planes, tok_rows, -1)

    def flip(array, mask):
        return lax.ppermute(array, "expert", pairs_flip(devices, mask))

    gathered = gathered.reshape(planes, 4, tok_rows, width)
    even = me % 2 == 0
    near_mask, far_mask = 4 << (bits - 2), 4 << (bits - 1)

    def first_steps(out):
        here = [out[0]]
        held = dict(enumerate(out))
        for bit in range(bits - 1):
            for r in sorted(held, reverse=True):
                if r >> bit & 1 and 4 * r != near_mask:
                    came = flip(held.pop(r), 4 << bit)
                    to = r ^ (1 << bit)
                    if to:
                        held[to] = add32(held[to], came).astype(jnp.bfloat16)
                    else:
                        here.append(came)
        return held[far_mask // 4], held[near_mask // 4], here

    def last_step(far, near, here):
        ways = [
            [(i, i ^ (far_mask if i % 2 == turn else near_mask)) for i in range(devices)]
            for turn in (0, 1)
        ]
        came = [
            lax.ppermute(jnp.where(even, far, near), "expert", ways[0]),
            lax.ppermute(jnp.where(even, near, far), "expert", ways[1]),
        ]
        return here + came

    def over_ring(array):
        shares = [array]
        for _ in range(groups - 1):
            shares.append(lax.ppermute(shares[-1], "group", ring))
        return shares

    def joined(shares):
        return jnp.concatenate(shares, axis=0)

    def blocks(p, column):
        return owns[p], siblings[p], column, over_core(column)

    count = len(PARTS)
    crossed = [over_column(own_shares[p]) for p in range(AHEAD)]
    hidden = hidden_rows(gathered, gate_up, gate, me, 0)
    hidden, crossed[0], gathered = tie((hidden, crossed[0], gathered))

    columns = [over_ring(crossed[0])]
    halves = [exchange(hidden)]
    hidden = hidden_rows(gathered, gate_up, gate, me, 1)
    hidden, columns, crossed, halves, own_shares = tie((hidden, columns, crossed, halves, own_shares))

    columns.append(over_ring(crossed[1]))
    if len(crossed) < 3:
        crossed.append(over_column(own_shares[2]))
    halves.append(exchange(hidden))
    terms = [
        jnp.concatenate([part.reshape(planes, -1, half) for part in parts], axis=1).reshape(-1, half)
        for parts in zip(*halves)
    ]
    out = second(terms, blocks(0, joined(columns[0])))

    totals = []
    before = None
    for w in range(count):
        out, columns, crossed, own_shares = tie((out, columns, crossed, own_shares))
        if w + 2 < count:
            columns.append(over_ring(crossed[w + 2]))
        if w + 3 < count:
            crossed.append(over_column(own_shares[w + 3]))
        far, near, here = first_steps(out)
        if before is not None:
            totals.append(add32(*last_step(*before)).astype(jnp.bfloat16))
        if w + 1 < count:
            out = second(terms, blocks(w + 1, joined(columns[w + 1])))
        far, near, here, totals[:-1] = tie((far, near, here, totals[:-1]))
        before = far, near, here
    totals.append(add32(*last_step(*before)).astype(jnp.bfloat16))
    return jnp.concatenate(totals, axis=1)


def solution(mesh):
    return jax.shard_map(
        per_device,
        mesh=mesh,
        in_specs=(
            P(("group", "expert"), None),
            P(("group", "expert"), None),
            P(("group", "expert"), None),
            P(),
            P("expert", None, None),
            P("expert", None, None),
        ),
        out_specs=P(("group", "expert"), None),
        check_vma=False,
    )
```

```python
import jax
import jax.numpy as jnp
from jax import lax
from jax.experimental import pallas as pl
from jax.experimental.pallas import tpu as pltpu
from jax.sharding import PartitionSpec as P

PARTS = (3, 3, 2)
AHEAD = 2
TILE = 256


def pairs_flip(devices, bits):
    return [(i, i ^ bits) for i in range(devices)]


def add32(*terms):
    total = terms[0].astype(jnp.float32)
    for term in terms[1:]:
        total = total + term.astype(jnp.float32)
    return total


def hidden_kernel(place, tokens, weight, gate, out):
    planes, _, rows, width = tokens.shape
    half = weight.shape[1] // 2

    @pl.loop(0, half // TILE)
    def _(n):
        first = pl.ds(pl.multiple_of(n * TILE, TILE), TILE)
        last = pl.ds(pl.multiple_of(half + n * TILE, TILE), TILE)
        x = tokens[:, 0].reshape(planes * rows, width)
        a = jnp.dot(x, weight[:, first], preferred_element_type=jnp.float32)
        b = jnp.dot(x, weight[:, last], preferred_element_type=jnp.float32)
        h = a / (1.0 + jnp.exp(-a)) * b
        h = h.reshape(planes, rows, TILE) * gate[:, 0]
        h = h.astype(out.dtype)
        for plane in range(planes):
            out[0, jnp.bitwise_xor(place[0], plane), :, first] = h[plane]


def hidden_rows(gathered, weight, gate, me, which):
    planes, _, rows, width = gathered.shape
    half = weight.shape[1] // 2
    block = rows // 2
    place = jnp.stack([me // 4, me % 4]).astype(jnp.int32)

    def source(flip, place):
        return (0, jnp.bitwise_xor(place[1], flip), which, 0)

    return pl.pallas_call(
        hidden_kernel,
        out_shape=jax.ShapeDtypeStruct((4, planes, block, half), jnp.bfloat16),
        grid_spec=pltpu.PrefetchScalarGridSpec(
            num_scalar_prefetch=1,
            grid=(4,),
            in_specs=[
                pl.BlockSpec((planes, 1, block, width), source),
                pl.BlockSpec(
                    weight.shape, lambda flip, place: (0, 0), pipeline_mode=pl.Buffered(1)
                ),
                pl.BlockSpec((planes, 1, block, 1), source),
            ],
            out_specs=pl.BlockSpec(
                (1, planes, block, half), lambda flip, place: (flip, 0, 0, 0)
            ),
        ),
        compiler_params=pltpu.CompilerParams(vmem_limit_bytes=44 * 1024 * 1024),
        cost_estimate=pl.CostEstimate(flops=4*planes*rows//2*width*2*half*2//1, bytes_accessed=2*width*2*half//1, transcendentals=0),
    )(place, gathered, weight, gate)


def sum_kernel(*refs):
    *pairs, out = refs
    half = len(pairs) // 2
    total = 0.0
    for term, weight in zip(pairs[:half], pairs[half:]):
        total = total + jnp.dot(term[...], weight[...], preferred_element_type=jnp.float32)
    out[...] = total.astype(out.dtype)


def sum_of_products(terms, weights):
    rows, depth = terms[0].shape
    width = weights[0].shape[1]
    tile = max(t for t in range(128, 897, 128) if width % t == 0)
    return pl.pallas_call(
        sum_kernel,
        out_shape=jax.ShapeDtypeStruct((rows, width), jnp.bfloat16),
        grid=(width // tile,),
        in_specs=[pl.BlockSpec((rows, depth), lambda i: (0, 0)) for _ in terms]
        + [pl.BlockSpec((depth, tile), lambda i: (0, i)) for _ in weights],
        out_specs=pl.BlockSpec((rows, tile), lambda i: (0, i)),
        compiler_params=pltpu.CompilerParams(vmem_limit_bytes=32 * 1024 * 1024),
        cost_estimate=pl.CostEstimate(flops=2*rows*4*depth*width//1, bytes_accessed=8*depth*width//1, transcendentals=0),
    )(*terms, *weights)


def per_device(tokens, expert_ids, gate_weights, slot_expert, w_gate_up, w_down):
    devices = lax.axis_size("expert")
    groups = lax.axis_size("group")
    planes = devices // 4
    bits = planes.bit_length() - 1
    tok_rows, width = tokens.shape
    top_count = expert_ids.shape[1]
    me = lax.axis_index("expert")
    gate_up = w_gate_up[0]
    down = w_down[0]
    half = down.shape[0]
    share = half // groups
    shift = lax.axis_index("group") * share
    ring = [(i, (i - 1) % groups) for i in range(groups)]
    tie = lax.optimization_barrier

    def over_core(array):
        return lax.ppermute(array, "expert", pairs_flip(devices, 1))

    def over_column(array):
        return lax.ppermute(array, "expert", pairs_flip(devices, 2))

    gathered = lax.all_gather(tokens, "expert", axis=0, tiled=True)
    routing = jnp.concatenate(
        [expert_ids.T.astype(jnp.float32), gate_weights.T], axis=0
    )
    routing = lax.all_gather(routing, "expert", axis=0, tiled=False)
    mine = slot_expert[me].astype(jnp.float32)
    gate = jnp.sum(
        jnp.where(routing[:, :top_count] == mine, routing[:, top_count:], 0.0), axis=1
    )
    gate = gate.reshape(planes, 4, tok_rows, 1)

    edges = [width * sum(PARTS[:p]) // 8 for p in range(len(PARTS) + 1)]
    owns = [down[:, edges[p] : edges[p + 1]] for p in range(len(PARTS))]
    own_share = lax.dynamic_slice_in_dim(down, shift, share, axis=0)
    own_shares = [own_share[:, edges[p] : edges[p + 1]] for p in range(len(PARTS))]
    siblings = [over_core(own) for own in owns]
    gathered, gate, siblings, own_shares = tie((gathered, gate, siblings, own_shares))

    def exchange(hidden):
        hidden = hidden.reshape(4, -1, half)
        terms = [hidden[0]]
        for bits in (1, 2, 3):
            term = lax.ppermute(hidden[bits], "expert", pairs_flip(devices, bits))
            if bits >= 2:
                term = lax.dynamic_slice_in_dim(
                    jnp.concatenate([term, term], axis=1), shift, half, axis=1
                )
            terms.append(term)
        return terms

    def second(terms, weight):
        return sum_of_products(terms, weight).reshape(planes, tok_rows, -1)

    def flip(array, mask):
        return lax.ppermute(array, "expert", pairs_flip(devices, mask))

    gathered = gathered.reshape(planes, 4, tok_rows, width)
    even = me % 2 == 0
    near_mask, far_mask = 4 << (bits - 2), 4 << (bits - 1)

    def first_steps(out, also):
        here = [out[0]]
        held = dict(enumerate(out))
        for bit in range(bits - 1):
            for r in sorted(held, reverse=True):
                if r >> bit & 1 and 4 * r != near_mask:
                    came = flip(held.pop(r), 4 << bit)
                    to = r ^ (1 << bit)
                    if to:
                        mine = held[to] if also is None else tie((held[to], also))[0]
                        held[to] = add32(mine, came).astype(jnp.bfloat16)
                    else:
                        here.append(came)
        return held[far_mask // 4], held[near_mask // 4], here

    def last_step(far, near, here):
        ways = [
            [(i, i ^ (far_mask if i % 2 == turn else near_mask)) for i in range(devices)]
            for turn in (0, 1)
        ]
        came = [
            lax.ppermute(jnp.where(even, far, near), "expert", ways[0]),
            lax.ppermute(jnp.where(even, near, far), "expert", ways[1]),
        ]
        return here + came

    def over_ring(array):
        shares = [array]
        for _ in range(groups - 1):
            shares.append(lax.ppermute(shares[-1], "group", ring))
        return shares

    def joined(shares):
        return jnp.concatenate(shares, axis=0)

    def blocks(p, column):
        return owns[p], siblings[p], column, over_core(column)

    count = len(PARTS)
    crossed = [over_column(own_shares[p]) for p in range(AHEAD)]
    hidden = hidden_rows(gathered, gate_up, gate, me, 0)
    hidden, crossed[0], gathered = tie((hidden, crossed[0], gathered))

    columns = [over_ring(crossed[0])]
    halves = [exchange(hidden)]
    hidden = hidden_rows(gathered, gate_up, gate, me, 1)
    hidden, columns, crossed, halves, own_shares = tie((hidden, columns, crossed, halves, own_shares))

    columns.append(over_ring(crossed[1]))
    if len(crossed) < 3:
        crossed.append(over_column(own_shares[2]))
    halves.append(exchange(hidden))
    terms = [
        jnp.concatenate([part.reshape(planes, -1, half) for part in parts], axis=1).reshape(-1, half)
        for parts in zip(*halves)
    ]
    out = second(terms, blocks(0, joined(columns[0])))

    totals = []
    before = None
    for w in range(count):
        out, columns, crossed, own_shares = tie((out, columns, crossed, own_shares))
        if w + 2 < count:
            columns.append(over_ring(crossed[w + 2]))
        if w + 3 < count:
            crossed.append(over_column(own_shares[w + 3]))
        if before is not None:
            totals.append(add32(*last_step(*before)).astype(jnp.bfloat16))
        if w + 1 < count:
            following = second(terms, blocks(w + 1, joined(columns[w + 1])))
        far, near, here = first_steps(out, following if 1 <= w and w + 1 < count else None)
        out = following
        far, near, here, totals[:-1] = tie((far, near, here, totals[:-1]))
        before = far, near, here
    totals.append(add32(*last_step(*before)).astype(jnp.bfloat16))
    return jnp.concatenate(totals, axis=1)


def solution(mesh):
    return jax.shard_map(
        per_device,
        mesh=mesh,
        in_specs=(
            P(("group", "expert"), None),
            P(("group", "expert"), None),
            P(("group", "expert"), None),
            P(),
            P("expert", None, None),
            P("expert", None, None),
        ),
        out_specs=P(("group", "expert"), None),
        check_vma=False,
    )
```
